128 devices in a mesh: row: 16 (over y, x_hi, core), col: 8 (over x_lo, z).
Axes of the slice: x: 4 (x_hi: 2, x_lo: 2; x = x_hi * 2 + x_lo), y: 4, z: 4, core: 2. Of those that a mesh axis runs over, the one named last changes fastest.
Arguments:
- inputs: bfloat16 [2048, 8192], P('row', 'col'), may hold values from -6 to 6
- cotangent: bfloat16 [2048, 8192], P('row', 'col'), may hold values from -6 to 6
- gate_pre: bfloat16 [2048, 14336], P('col', 'row'), may hold values from -8 to 8
- up_pre: bfloat16 [2048, 14336], P('col', 'row'), may hold values from -6 to 6
- w_gate: bfloat16 [8192, 14336], P('col', 'row'), may hold values from -0.0625 to 0.0625
- w_up: bfloat16 [8192, 14336], P('col', 'row'), may hold values from -0.0625 to 0.0625
- w_down: bfloat16 [14336, 8192], P('row', 'col'), may hold values from -0.046875 to 0.046875
Outputs:
- grad_inputs: bfloat16 [2048, 8192], P('row', 'col')
- grad_w_gate: bfloat16 [8192, 14336], P('col', 'row')
- grad_w_up: bfloat16 [8192, 14336], P('col', 'row')
- grad_w_down: bfloat16 [14336, 8192], P('row', 'col')
The draws below stay inside these ranges and needn't reach their ends.
All inputs are finite; a program needn't handle non-finite values.
Results may differ from the reference program's by a relative error of at most 0.03.
Values may be sent and summed in bfloat16 or wider, within the bound.
A program may use at most 128 MiB of HBM per device.

```python
import jax
import jax.numpy as jnp
from jax import lax

D = 8192
FF = 14336
TOKENS = 2048
N_ROW = 16
N_COL = 8


def shard_levels(stream_key, dims, pieces, smallest, high):
    level = 1.0
    for dim, shards_of in pieces:
        draws = jax.random.uniform(jax.random.fold_in(jax.random.fold_in(stream_key, 6), dim), (shards_of,), jnp.float32, smallest / len(pieces), high / len(pieces))
        level = level * jnp.repeat(jnp.exp(draws), dims[dim] // shards_of).reshape((-1,) + (1,) * (len(dims) - 1 - dim))
    return level


def noise(rng, shape, spread, reach, shards=(), kind=jnp.bfloat16):
    factor_of = shard_levels(rng, shape, shards, -0.22, 0.18) if shards else 1.0
    entries = jax.random.normal(rng, shape, jnp.float32) * spread * factor_of
    return jnp.minimum(jnp.maximum(entries, -reach), reach).astype(kind)


def setup_inputs(seed: int = 0) -> dict:
    key_list = jax.random.split(jax.random.key(seed), 8)
    inputs = noise(key_list[0], (TOKENS, D), 1.0, 6.0, ((0, 16), (1, 8)))
    cotangent = noise(key_list[1], (TOKENS, D), 1.0, 6.0, ((0, 16), (1, 8)))
    gate_pre = noise(key_list[2], (TOKENS, FF), 1.5, 8.0, ((0, 8), (1, 16)))
    up_pre = noise(key_list[3], (TOKENS, FF), 1.0, 6.0, ((0, 8), (1, 16)))
    w_gate = noise(key_list[4], (D, FF), D ** -0.5, 0.0625, ((0, 8), (1, 16)))
    w_up = noise(key_list[5], (D, FF), D ** -0.5, 0.0625, ((0, 8), (1, 16)))
    w_down = noise(key_list[6], (FF, D), FF ** -0.5, 0.046875, ((0, 16), (1, 8)))
    return dict(inputs=inputs, cotangent=cotangent, gate_pre=gate_pre, up_pre=up_pre, w_gate=w_gate, w_up=w_up, w_down=w_down)


def swiglu_back(gate_pre, up_pre, grad_hidden):
    gate = gate_pre.astype(jnp.float32)
    up = up_pre.astype(jnp.float32)
    sigma = jax.nn.sigmoid(gate)
    silu = gate * sigma
    hidden = (silu * up).astype(jnp.bfloat16)
    grad_gate = (grad_hidden * up * sigma * (1.0 + gate * (1.0 - sigma))).astype(jnp.bfloat16)
    grad_up = (grad_hidden * silu).astype(jnp.bfloat16)
    return hidden, grad_gate, grad_up


def reference(inputs, cotangent, gate_pre, up_pre, w_gate, w_up, w_down):
    across = (((1,), (1,)), ((), ()))
    along = (((0,), (0,)), ((), ()))
    width_block = D // N_COL
    unit_block = FF // N_ROW

    def hidden_step(total, index):
        start = (index * width_block).astype(jnp.int32)
        left = lax.dynamic_slice_in_dim(cotangent, start, width_block, 1)
        right = lax.dynamic_slice_in_dim(w_down, start, width_block, 1)
        part = lax.dot_general(left, right, across, preferred_element_type=jnp.float32)
        part = lax.optimization_barrier(part.astype(jnp.bfloat16)).astype(jnp.float32)
        return total + part, None

    grad_hidden, _ = lax.scan(hidden_step, jnp.zeros((TOKENS, FF), jnp.float32), jnp.arange(N_COL, dtype=jnp.int32))
    hidden, grad_gate, grad_up = swiglu_back(gate_pre, up_pre, grad_hidden)
    grad_w_down = lax.dot_general(hidden, cotangent, along, preferred_element_type=jnp.float32).astype(jnp.bfloat16)
    grad_w_gate = lax.dot_general(inputs, grad_gate, along, preferred_element_type=jnp.float32).astype(jnp.bfloat16)
    grad_w_up = lax.dot_general(inputs, grad_up, along, preferred_element_type=jnp.float32).astype(jnp.bfloat16)

    def input_step(total, index):
        start = (index * unit_block).astype(jnp.int32)
        gate_part = lax.dynamic_slice_in_dim(grad_gate, start, unit_block, 1)
        up_part = lax.dynamic_slice_in_dim(grad_up, start, unit_block, 1)
        gate_w = lax.dynamic_slice_in_dim(w_gate, start, unit_block, 1)
        up_w = lax.dynamic_slice_in_dim(w_up, start, unit_block, 1)
        part = lax.dot_general(gate_part, gate_w, across, preferred_element_type=jnp.float32)
        part = part + lax.dot_general(up_part, up_w, across, preferred_element_type=jnp.float32)
        part = lax.optimization_barrier(part.astype(jnp.bfloat16)).astype(jnp.float32)
        return total + part, None

    grad_inputs, _ = lax.scan(input_step, jnp.zeros((TOKENS, D), jnp.float32), jnp.arange(N_ROW, dtype=jnp.int32))
    return grad_inputs.astype(jnp.bfloat16), grad_w_gate, grad_w_up, grad_w_down
```

```python
import functools

import jax
import jax.numpy as jnp
from jax import lax
from jax.experimental import pallas as pl
from jax.experimental.pallas import tpu as pltpu
from jax.sharding import PartitionSpec as P

MESH = pl.DeviceIdType.MESH
BF16 = jnp.bfloat16
F32 = jnp.float32
ACROSS = (((1,), (1,)), ((), ()))

ROWS = 128
TOK = 256
HALF = 128
D = 1024
F = 896

N_ROWS = 17
N_HID = 8
N_GH = 14
N_G = 14
COT0 = 0
INP0 = COT0 + N_ROWS
HID0 = INP0 + N_ROWS
GH0 = HID0 + N_HID
G0 = GH0 + N_GH
PAIR0 = G0 + N_G
N_SEM = PAIR0 + 8


def kernel(
    inp_hbm, cot_hbm, gate_hbm, up_hbm, wg_hbm, wu_hbm, wd_hbm,
    gi_hbm, dwg_hbm, dwu_hbm, dwd_hbm,
    cot, inp_t, hid_t, grads, w_in, wd, inp_own, gate, up,
    slope, silu, gh_send, gh_recv, gh_keep, gh_own,
    gi_part, pair_send, pair_recv, q_send, q_recv,
    dw, dwd, gi_out,
    send_sem, recv_sem, q_send_sem, q_recv_sem, local_sem, out_sem,
):
    r = lax.axis_index("row")
    c = lax.axis_index("col")
    core = lax.rem(r, 2)
    chip = lax.div(r, 2)
    xh = lax.rem(chip, 2)
    y = lax.div(chip, 2)
    xl = lax.div(c, 4)
    z = lax.rem(c, 4)

    def row_of(y_, xh_, core_):
        return (y_ * 2 + xh_) * 2 + core_

    y_up, y_dn, y_far = lax.rem(y + 1, 4), lax.rem(y + 3, 4), lax.rem(y + 2, 4)
    z_up, z_dn, z_far = lax.rem(z + 1, 4), lax.rem(z + 3, 4), lax.rem(z + 2, 4)
    xo = 1 - xl
    xho = 1 - xh
    c_xl = xo * 4 + z

    to_yp = (row_of(y_up, xh, core), c)
    to_ym = (row_of(y_dn, xh, core), c)
    to_xh = (row_of(y, xho, core), c)
    to_core = (row_of(y, xh, 1 - core), c)
    to_zp = (r, xl * 4 + z_up)
    to_zm = (r, xl * 4 + z_dn)
    to_xl = (r, c_xl)

    def local(i, src, dst):
        return pltpu.make_async_copy(src, dst, local_sem.at[i])

    def tile(start, size, step):
        return pl.ds(pl.multiple_of(start, step), size)

    def rows(r_):
        return tile(r_ * ROWS, ROWS, ROWS)

    def toks(c_):
        return tile(c_ * TOK, TOK, TOK)

    def halves(c_, h):
        return tile(c_ * TOK + h * HALF, HALF, HALF)

    loads = [
        local(0, cot_hbm, cot.at[rows(r), :]),
        local(1, gate_hbm, gate),
        local(2, up_hbm, up),
        local(3, inp_hbm, inp_own),
        local(4, wd_hbm, wd),
        local(5, wg_hbm, w_in.at[:, pl.ds(0, F)]),
        local(6, wu_hbm, w_in.at[:, pl.ds(F, F)]),
    ]
    for load in loads:
        load.start()

    barrier = pltpu.get_barrier_semaphore()
    partners = [to_yp, to_ym, to_xh, to_core, to_zp, to_zm, to_xl]
    for device in partners:
        pl.semaphore_signal(barrier, inc=1, device_id=device, device_id_type=MESH)
    far = [
        (row_of(y_far, xh, core), c),
        (row_of(y_up, xho, core), c),
        (row_of(y_dn, xho, core), c),
        (row_of(y_far, xho, core), c),
    ]
    for device in far:
        pl.semaphore_signal(barrier, inc=1, device_id=device, device_id_type=MESH)
    pl.semaphore_wait(barrier, len(partners) + len(far))

    started = []

    def message(i, src, dst, device):
        return pltpu.make_async_remote_copy(
            src_ref=src,
            dst_ref=dst,
            send_sem=send_sem.at[i],
            recv_sem=recv_sem.at[i],
            device_id=device,
            device_id_type=MESH,
        )

    def send(m):
        m.start()
        started.append(m)

    def row_gather(base, at):
        m = {}

        def add(name, i, y_, xh_, part, device):
            ref = at(y_, xh_, part)
            m[name] = message(base + i, ref, ref, device)

        add("own>xh", 0, y, xh, None, to_xh)
        add("own>y+", 1, y, xh, None, to_yp)
        add("own>y-", 2, y, xh, None, to_ym)
        add("xh>y+", 3, y, xho, None, to_yp)
        add("xh>y-", 4, y, xho, None, to_ym)
        add("own2>y+", 5, y_dn, xh, 0, to_yp)
        add("own2>y-", 6, y_up, xh, 1, to_ym)
        add("xh2>y+", 7, y_dn, xho, 0, to_yp)
        add("xh2>y-", 8, y_up, xho, 1, to_ym)
        k = 9
        for yn, y_ in (("0", y), ("-", y_dn), ("+", y_up), ("f", y_far)):
            for xn, xh_ in (("own", xh), ("xh", xho)):
                add(xn + yn + ">core", k, y_, xh_, None, to_core)
                k += 1
        return m

    def cot_at(y_, xh_, part):
        start = row_of(y_, xh_, core) * ROWS
        if part is None:
            return cot.at[tile(start, ROWS, ROWS), :]
        return cot.at[tile(start + part * (ROWS // 2), ROWS // 2, ROWS // 2), :]

    def inp_at(y_, xh_, part):
        cols = tile(row_of(y_, xh_, core) * ROWS, ROWS, ROWS)
        if part is None:
            return inp_t.at[:, cols]
        return inp_t.at[pl.ds(part * (D // 2), D // 2), cols]

    cm = row_gather(COT0, cot_at)
    im = row_gather(INP0, inp_at)

    def row_start(m):
        send(m["own>xh"])
        send(m["own>y+"])
        send(m["own>y-"])
        send(m["own0>core"])

    def row_xh(m):
        m["own>xh"].wait_recv()
        send(m["xh>y+"])
        send(m["xh>y-"])
        send(m["xh0>core"])

    def row_near(m, which):
        m[which + ">y+"].wait_recv()
        send(m[which + "2>y+"])
        send(m[which + "->core"])
        m[which + ">y-"].wait_recv()
        send(m[which + "2>y-"])
        send(m[which + "+>core"])

    def row_far(m, which):
        m[which + "2>y+"].wait_recv()
        m[which + "2>y-"].wait_recv()
        send(m[which + "f>core"])

    def row_finish(m):
        for name in m:
            if name.endswith(">core"):
                m[name].wait_recv()

    loads[0].wait()
    row_start(cm)
    loads[1].wait()
    loads[2].wait()

    def activate(t, _):
        part = pl.ds(pl.multiple_of(t * 16, 16), 16)
        g = gate[part, :].astype(F32)
        u = up[part, :].astype(F32)
        s = 1.0 / (1.0 + jnp.exp(-g))
        sl = g * s
        silu[part, :] = sl
        slope[part, :] = u * s * (1.0 + g * (1.0 - s))
        gh_own[part, :] = sl * u
        return 0

    lax.fori_loop(0, TOK // 16, activate, 0)

    def turn(t, _):
        part = pl.ds(pl.multiple_of(t * 128, 128), 128)
        hid_t[part, toks(c)] = gh_own[:, part].T.astype(BF16)
        return 0

    lax.fori_loop(0, F // 128, turn, 0)

    def hid_at(c_, part):
        if part is None:
            return hid_t.at[:, toks(c_)]
        return hid_t.at[pl.ds(part * (F // 2), F // 2), toks(c_)]

    hm = {}

    def hid_add(name, i, c_, part, device):
        ref = hid_at(c_, part)
        hm[name] = message(HID0 + i, ref, ref, device)

    c_zp, c_zm, c_zf = xl * 4 + z_up, xl * 4 + z_dn, xl * 4 + z_far
    hid_add("own>z+", 0, c, None, to_zp)
    hid_add("own>z-", 1, c, None, to_zm)
    hid_add("own>xl", 2, c, None, to_xl)
    hid_add("far>z+", 3, c_zm, 0, to_zp)
    hid_add("far>z-", 4, c_zp, 1, to_zm)
    hid_add("zm>xl", 5, c_zm, None, to_xl)
    hid_add("zp>xl", 6, c_zp, None, to_xl)
    hid_add("zf>xl", 7, c_zf, None, to_xl)
    send(hm["own>z+"])
    send(hm["own>z-"])
    send(hm["own>xl"])

    loads[3].wait()

    def turn_inp(t, _):
        part = pl.ds(pl.multiple_of(t * 128, 128), 128)
        inp_t[part, rows(r)] = inp_own[:, part].astype(F32).T.astype(BF16)
        return 0

    lax.fori_loop(0, D // 128, turn_inp, 0)

    row_xh(cm)
    row_near(cm, "own")
    hm["own>z+"].wait_recv()
    send(hm["far>z+"])
    send(hm["zm>xl"])
    hm["own>z-"].wait_recv()
    send(hm["far>z-"])
    send(hm["zp>xl"])
    row_near(cm, "xh")
    row_start(im)
    row_far(cm, "own")
    row_far(cm, "xh")
    hm["far>z+"].wait_recv()
    hm["far>z-"].wait_recv()
    send(hm["zf>xl"])
    row_finish(cm)
    loads[4].wait()

    def gh_dot(c_):
        return lax.dot_general(cot[toks(c_), :], wd[...], ACROSS, preferred_element_type=F32)

    gm = {}

    def gh_add(name, i, device):
        gm[name] = message(GH0 + i, gh_send.at[i], gh_recv.at[i], device)

    for k, who in enumerate(("other", "own")):
        gh_add("relay+" + who, 0 + k, to_zp)
        gh_add("relay-" + who, 2 + k, to_zm)
        gh_add("direct+" + who, 4 + k, to_zp)
        gh_add("direct-" + who, 6 + k, to_zm)
        gh_add("comb+" + who, 8 + k, to_zp)
        gh_add("comb-" + who, 10 + k, to_zm)
        gh_add("xl%d" % k, 12 + k, to_xl)
    sides = (("other", 0, xo), ("own", 1, xl))

    for who, k, x_ in sides:
        part = gh_dot(x_ * 4 + z_far).astype(BF16)
        gh_send[0 + k] = part[:HALF]
        gh_send[2 + k] = part[HALF:]
        send(gm["relay+" + who])
        send(gm["relay-" + who])
    for who, k, x_ in sides:
        part = gh_dot(x_ * 4 + z_up)
        gh_send[4 + k] = part[HALF:].astype(BF16)
        gh_keep[k] = part[:HALF]
        send(gm["direct+" + who])
        part = gh_dot(x_ * 4 + z_dn)
        gh_send[6 + k] = part[:HALF].astype(BF16)
        gh_keep[2 + k] = part[HALF:]
        send(gm["direct-" + who])
    gh_own[...] = gh_dot(xo * 4 + z)
    row_xh(im)
    for who, k, x_ in sides:
        gm["relay+" + who].wait_recv()
        gh_send[8 + k] = (gh_keep[k] + gh_recv[0 + k].astype(F32)).astype(BF16)
        send(gm["comb+" + who])
        gm["relay-" + who].wait_recv()
        gh_send[10 + k] = (gh_keep[2 + k] + gh_recv[2 + k].astype(F32)).astype(BF16)
        send(gm["comb-" + who])
    row_near(im, "own")
    row_near(im, "xh")
    gm["direct+other"].wait_recv()
    gm["direct-other"].wait_recv()
    gm["comb+other"].wait_recv()
    gm["comb-other"].wait_recv()
    gh_send[12] = (
        gh_own[pl.ds(0, HALF), :] + gh_recv[6].astype(F32) + gh_recv[8].astype(F32)
    ).astype(BF16)
    send(gm["xl0"])
    gh_send[13] = (
        gh_own[pl.ds(HALF, HALF), :] + gh_recv[4].astype(F32) + gh_recv[10].astype(F32)
    ).astype(BF16)
    send(gm["xl1"])
    gh_own[...] = gh_dot(c)
    row_far(im, "own")
    row_far(im, "xh")
    gm["direct+own"].wait_recv()
    gm["direct-own"].wait_recv()
    gm["comb+own"].wait_recv()
    gm["comb-own"].wait_recv()

    gg = {}

    def g_add(name, i, c_, h, device):
        ref = grads.at[halves(c_, h), :]
        gg[name] = message(G0 + i, ref, ref, device)

    c_xzp, c_xzm, c_xzf = xo * 4 + z_up, xo * 4 + z_dn, xo * 4 + z_far
    for h in (0, 1):
        g_add("own%d>z+" % h, 0 + h, c, h, to_zp)
        g_add("own%d>z-" % h, 2 + h, c, h, to_zm)
        g_add("own%d>xl" % h, 4 + h, c, h, to_xl)
        g_add("xl%d>z+" % h, 6 + h, c_xl, h, to_zp)
        g_add("xl%d>z-" % h, 8 + h, c_xl, h, to_zm)
    g_add("far>z+", 10, c_zm, 0, to_zp)
    g_add("far>z-", 11, c_zp, 1, to_zm)
    g_add("xfar>z+", 12, c_xzm, 0, to_zp)
    g_add("xfar>z-", 13, c_xzp, 1, to_zm)

    for h in (0, 1):
        gm["xl%d" % h].wait_recv()
        a, b = ((6, 8), (4, 10))[h]

        def grad(t, _, h=h, a=a, b=b):
            here = pl.ds(pl.multiple_of(t * 16, 16), 16)
            part = pl.ds(pl.multiple_of(h * HALF + t * 16, 16), 16)
            gh = (
                gh_own[part, :]
                + gh_recv[a + 1, here, :].astype(F32)
                + gh_recv[b + 1, here, :].astype(F32)
                + gh_recv[12 + h, here, :].astype(F32)
            )
            dst = tile(c * TOK + h * HALF + t * 16, 16, 16)
            grads[dst, pl.ds(0, F)] = (gh * slope[part, :]).astype(BF16)
            grads[dst, pl.ds(F, F)] = (gh * silu[part, :]).astype(BF16)
            return 0

        lax.fori_loop(0, HALF // 16, grad, 0)
        send(gg["own%d>z+" % h])
        send(gg["own%d>z-" % h])
        send(gg["own%d>xl" % h])

    loads[5].wait()
    loads[6].wait()

    pairs = []
    sums = []

    def gi_make(c_):
        i = len(pairs)
        gi_part[i % 2] = lax.dot_general(
            grads[toks(c_), :], w_in[...], ACROSS, preferred_element_type=F32
        )
        theirs = tile((1 - core) * ROWS, ROWS, ROWS)
        pair_send[i] = gi_part[i % 2, theirs, :].astype(BF16)
        m = message(PAIR0 + i, pair_send.at[i], pair_recv.at[i], to_core)
        send(m)
        pairs.append((m, c_))

    def gi_sum():
        i = len(sums)
        m, c_ = pairs[i]
        m.wait_recv()
        mine = tile(core * ROWS, ROWS, ROWS)
        total = (gi_part[i % 2, mine, :] + pair_recv[i].astype(F32)).astype(BF16)
        q_send[i] = total
        q = pltpu.make_async_remote_copy(
            src_ref=q_send.at[i],
            dst_ref=q_recv.at[chip],
            send_sem=q_send_sem.at[i],
            recv_sem=q_recv_sem.at[chip],
            device_id=(c_ * 2 + core, c),
            device_id_type=MESH,
        )
        here = c_ == chip

        @pl.when(jnp.logical_not(here))
        def _():
            q.start()

        @pl.when(here)
        def _():
            q_recv[chip] = q_send[i]

        sums.append((q, here))

    gi_make(c)

    row_finish(im)
    for name in ("own>xl", "zm>xl", "zp>xl", "zf>xl"):
        hm[name].wait_recv()

    gg["own0>xl"].wait_recv()
    send(gg["xl0>z+"])
    send(gg["xl0>z-"])
    gg["own0>z+"].wait_recv()
    send(gg["far>z+"])
    gg["own0>z-"].wait_recv()

    def down(t, _):
        part = pl.ds(pl.multiple_of(t * 224, 32), 224)
        dwd[part, :] = jnp.dot(
            hid_t[part, :], cot[...], preferred_element_type=F32
        ).astype(BF16)
        return 0

    lax.fori_loop(0, 4, down, 0)
    outs = [pltpu.make_async_copy(dwd, dwd_hbm, out_sem.at[0])]
    outs[0].start()

    gg["own1>xl"].wait_recv()
    send(gg["xl1>z+"])
    send(gg["xl1>z-"])
    gi_make(c_xl)
    gi_sum()
    gg["own1>z-"].wait_recv()
    send(gg["far>z-"])
    gg["own1>z+"].wait_recv()
    gi_make(c_zm)
    gi_sum()
    gi_make(c_zp)
    gi_sum()
    gg["xl0>z+"].wait_recv()
    send(gg["xfar>z+"])
    gg["xl0>z-"].wait_recv()
    gg["xl1>z-"].wait_recv()
    send(gg["xfar>z-"])
    gg["xl1>z+"].wait_recv()
    gi_make(c_xzm)
    gi_sum()
    gi_make(c_xzp)
    gi_sum()
    gg["far>z+"].wait_recv()
    gg["far>z-"].wait_recv()
    gi_make(c_zf)
    gi_sum()
    gg["xfar>z+"].wait_recv()
    gg["xfar>z-"].wait_recv()
    gi_make(c_xzf)
    gi_sum()
    gi_sum()

    for k, dst in ((0, dwg_hbm), (1, dwu_hbm)):

        def inward(t, _, k=k):
            part = pl.ds(pl.multiple_of(t * 256, 256), 256)
            dw[k, part, :] = jnp.dot(
                inp_t[part, :], grads[:, pl.ds(k * F, F)], preferred_element_type=F32
            ).astype(BF16)
            return 0

        lax.fori_loop(0, 4, inward, 0)
        copy = pltpu.make_async_copy(dw.at[k], dst, out_sem.at[1 + k])
        copy.start()
        outs.append(copy)

    for j in range(8):
        arrival = pltpu.make_async_remote_copy(
            src_ref=q_send.at[j],
            dst_ref=q_recv.at[j],
            send_sem=q_send_sem.at[j],
            recv_sem=q_recv_sem.at[j],
            device_id=to_core,
            device_id_type=MESH,
        )

        @pl.when(chip != j)
        def _():
            arrival.wait_recv()

    def finish(t, _):
        part = pl.ds(pl.multiple_of(t * 16, 16), 16)
        total = q_recv[0, part, :].astype(F32)
        for j in range(1, 8):
            total = total + q_recv[j, part, :].astype(F32)
        gi_out[part, :] = total.astype(BF16)
        return 0

    lax.fori_loop(0, ROWS // 16, finish, 0)
    copy = pltpu.make_async_copy(gi_out, gi_hbm, out_sem.at[3])
    copy.start()
    outs.append(copy)
    for m in started:
        m.wait_send()
    for q, here in sums:

        @pl.when(jnp.logical_not(here))
        def _():
            q.wait_send()

    for copy in outs:
        copy.wait()


def shards(inputs, cotangent, gate_pre, up_pre, w_gate, w_up, w_down):
    anywhere = pl.BlockSpec(memory_space=pl.ANY)
    vmem = pltpu.VMEM
    dma = pltpu.SemaphoreType.DMA
    return pl.pallas_call(
        kernel,
        out_shape=(
            jax.ShapeDtypeStruct((ROWS, D), BF16),
            jax.ShapeDtypeStruct((D, F), BF16),
            jax.ShapeDtypeStruct((D, F), BF16),
            jax.ShapeDtypeStruct((F, D), BF16),
        ),
        in_specs=[anywhere] * 7,
        out_specs=(anywhere,) * 4,
        scratch_shapes=[
            vmem((2048, D), BF16),
            vmem((D, 2048), BF16),
            vmem((F, 2048), BF16),
            vmem((2048, 2 * F), BF16),
            vmem((D, 2 * F), BF16),
            vmem((F, D), BF16),
            vmem((ROWS, D), BF16),
            vmem((TOK, F), BF16),
            vmem((TOK, F), BF16),
            vmem((TOK, F), F32),
            vmem((TOK, F), F32),
            vmem((14, HALF, F), BF16),
            vmem((14, HALF, F), BF16),
            vmem((4, HALF, F), F32),
            vmem((TOK, F), F32),
            vmem((2, TOK, D), F32),
            vmem((8, ROWS, D), BF16),
            vmem((8, ROWS, D), BF16),
            vmem((8, ROWS, D), BF16),
            vmem((8, ROWS, D), BF16),
            vmem((2, D, F), BF16),
            vmem((F, D), BF16),
            vmem((ROWS, D), BF16),
            dma((N_SEM,)),
            dma((N_SEM,)),
            dma((8,)),
            dma((8,)),
            dma((7,)),
            dma((4,)),
        ],
        compiler_params=pltpu.CompilerParams(
            collective_id=0, has_side_effects=True, vmem_limit_bytes=60 * 2**20
        ),
    )(inputs, cotangent, gate_pre, up_pre, w_gate, w_up, w_down)


def solution(mesh):
    placed = (
        P("row", "col"),
        P("row", "col"),
        P("col", "row"),
        P("col", "row"),
        P("col", "row"),
        P("col", "row"),
        P("row", "col"),
    )
    return jax.shard_map(
        shards,
        mesh=mesh,
        in_specs=placed,
        out_specs=(P("row", "col"), P("col", "row"), P("col", "row"), P("row", "col")),
        check_vma=False,
    )
```

```python
import functools

import jax
import jax.numpy as jnp
from jax import lax
from jax.experimental import pallas as pl
from jax.experimental.pallas import tpu as pltpu
from jax.sharding import PartitionSpec as P

MESH = pl.DeviceIdType.MESH
BF16 = jnp.bfloat16
F32 = jnp.float32
ACROSS = (((1,), (1,)), ((), ()))

ROWS = 128
TOK = 256
HALF = 128
FWD = 48
LATE = 32
D = 1024
F = 896

N_ROWS = 17
N_HID = 17
N_GH = 14
N_G = 30
COT0 = 0
INP0 = COT0 + N_ROWS
HID0 = INP0 + N_ROWS
GH0 = HID0 + N_HID
G0 = GH0 + N_GH
PAIR0 = G0 + N_G
N_FWD = 3
FWD0 = PAIR0 + 9
N_SEM = FWD0 + N_FWD
PARTS = 4


def kernel(
    inp_hbm, cot_hbm, gate_hbm, up_hbm, wg_hbm, wu_hbm, wd_hbm,
    gi_hbm, dwg_hbm, dwu_hbm, dwd_hbm,
    cot, inp_t, hid_t, grads, w_in, wd, inp_own, gate, up,
    slope, silu, gh_send, gh_recv, gh_keep, gh_own,
    gi_part, pair_send, pair_recv, q_send, q_recv, x_send, x_recv,
    dw, dw_sum, dwd, gi_out,
    send_sem, recv_sem, q_send_sem, q_recv_sem, q_late_sem, local_sem, out_sem,
):
    r = lax.axis_index("row")
    c = lax.axis_index("col")
    core = lax.rem(r, 2)
    chip = lax.div(r, 2)
    xh = lax.rem(chip, 2)
    y = lax.div(chip, 2)
    xl = lax.div(c, 4)
    z = lax.rem(c, 4)

    def row_of(y_, xh_, core_):
        return (y_ * 2 + xh_) * 2 + core_

    y_up, y_dn, y_far = lax.rem(y + 1, 4), lax.rem(y + 3, 4), lax.rem(y + 2, 4)
    z_up, z_dn, z_far = lax.rem(z + 1, 4), lax.rem(z + 3, 4), lax.rem(z + 2, 4)
    xo = 1 - xl
    xho = 1 - xh
    c_xl = xo * 4 + z

    to_yp = (row_of(y_up, xh, core), c)
    to_ym = (row_of(y_dn, xh, core), c)
    to_xh = (row_of(y, xho, core), c)
    to_core = (row_of(y, xh, 1 - core), c)
    to_zp = (r, xl * 4 + z_up)
    to_zm = (r, xl * 4 + z_dn)
    to_xl = (r, c_xl)

    def local(i, src, dst):
        return pltpu.make_async_copy(src, dst, local_sem.at[i])

    def tile(start, size, step):
        return pl.ds(pl.multiple_of(start, step), size)

    def rows(r_):
        return tile(r_ * ROWS, ROWS, ROWS)

    def toks(c_):
        return tile(c_ * TOK, TOK, TOK)

    def halves(c_, h):
        return tile(c_ * TOK + h * HALF, HALF, HALF)

    loads = [
        local(0, cot_hbm, cot.at[rows(r), :]),
        local(1, gate_hbm, gate),
        local(2, up_hbm, up),
        local(3, inp_hbm, inp_own),
        local(4, wd_hbm, wd),
        local(5, wg_hbm, w_in.at[:, pl.ds(0, F)]),
        local(6, wu_hbm, w_in.at[:, pl.ds(F, F)]),
    ]
    for load in loads:
        load.start()

    barrier = pltpu.get_barrier_semaphore()
    partners = [to_yp, to_ym, to_xh, to_core, to_zp, to_zm, to_xl]
    for device in partners:
        pl.semaphore_signal(barrier, inc=1, device_id=device, device_id_type=MESH)
    far = [
        (row_of(y_far, xh, core), c),
        (row_of(y_up, xho, core), c),
        (row_of(y_dn, xho, core), c),
        (row_of(y_far, xho, core), c),
    ]
    for device in far:
        pl.semaphore_signal(barrier, inc=1, device_id=device, device_id_type=MESH)
    pl.semaphore_wait(barrier, len(partners) + len(far))

    started = []

    def message(i, src, dst, device):
        return pltpu.make_async_remote_copy(
            src_ref=src,
            dst_ref=dst,
            send_sem=send_sem.at[i],
            recv_sem=recv_sem.at[i],
            device_id=device,
            device_id_type=MESH,
        )

    def send(m):
        m.start()
        started.append(m)

    def row_gather(base, at):
        m = {}

        def add(name, i, y_, xh_, part, device):
            ref = at(y_, xh_, part)
            m[name] = message(base + i, ref, ref, device)

        add("oh", 0, y, xh, None, to_xh)
        add("oy+", 1, y, xh, None, to_yp)
        add("oy-", 2, y, xh, None, to_ym)
        add("hy+", 3, y, xho, None, to_yp)
        add("hy-", 4, y, xho, None, to_ym)
        add("o2y+", 5, y_dn, xh, 0, to_yp)
        add("o2y-", 6, y_up, xh, 1, to_ym)
        add("h2y+", 7, y_dn, xho, 0, to_yp)
        add("h2y-", 8, y_up, xho, 1, to_ym)
        k = 9
        for yn, y_ in (("0", y), ("-", y_dn), ("+", y_up), ("f", y_far)):
            for xn, xh_ in (("o", xh), ("h", xho)):
                add(xn + yn + "c", k, y_, xh_, None, to_core)
                k += 1
        return m

    def cot_at(y_, xh_, part):
        start = row_of(y_, xh_, core) * ROWS
        if part is None:
            return cot.at[tile(start, ROWS, ROWS), :]
        return cot.at[tile(start + part * (ROWS // 2), ROWS // 2, ROWS // 2), :]

    def inp_at(y_, xh_, part):
        cols = tile(row_of(y_, xh_, core) * ROWS, ROWS, ROWS)
        if part is None:
            return inp_t.at[:, cols]
        return inp_t.at[pl.ds(part * (D // 2), D // 2), cols]

    cm = row_gather(COT0, cot_at)
    im = row_gather(INP0, inp_at)

    def row_start(m):
        send(m["oh"])
        send(m["oy+"])
        send(m["oy-"])
        send(m["o0c"])

    def row_xh(m):
        m["oh"].wait_recv()
        send(m["hy+"])
        send(m["hy-"])
        send(m["h0c"])

    def row_near(m, which):
        m[which + "y+"].wait_recv()
        send(m[which + "2y+"])
        send(m[which + "-c"])
        m[which + "y-"].wait_recv()
        send(m[which + "2y-"])
        send(m[which + "+c"])

    def row_far(m, which):
        m[which + "2y+"].wait_recv()
        m[which + "2y-"].wait_recv()
        send(m[which + "fc"])

    def row_finish(m):
        for name in m:
            if name.endswith("c"):
                m[name].wait_recv()

    loads[0].wait()
    row_start(cm)
    loads[1].wait()
    loads[2].wait()

    def activate(t, _):
        part = pl.ds(pl.multiple_of(t * 16, 16), 16)
        g = gate[part, :].astype(F32)
        u = up[part, :].astype(F32)
        s = 1.0 / (1.0 + jnp.exp(-g))
        sl = g * s
        silu[part, :] = sl
        slope[part, :] = u * s * (1.0 + g * (1.0 - s))
        gh_own[part, :] = sl * u
        return 0

    lax.fori_loop(0, TOK // 16, activate, 0)

    def turn(t, _):
        part = pl.ds(pl.multiple_of(t * 128, 128), 128)
        hid_t[part, toks(c)] = gh_own[:, part].T.astype(BF16)
        return 0

    lax.fori_loop(0, F // 128, turn, 0)

    def hid_add(name, c_, start, size, device):
        ref = hid_t.at[pl.ds(start, size), toks(c_)]
        hm[name] = message(HID0 + len(hm), ref, ref, device)

    hm = {}
    c_zp, c_zm, c_zf = xl * 4 + z_up, xl * 4 + z_dn, xl * 4 + z_far
    c_xzp, c_xzm, c_xzf = xo * 4 + z_up, xo * 4 + z_dn, xo * 4 + z_far
    A, B = F // 2, F // 4
    for way, device in (("z+", to_zp), ("z-", to_zm), ("x", to_xl)):
        hid_add("o0" + way, c, 0, A, device)
        hid_add("o1" + way, c, A, A, device)
    for way, near, xnear, at, device in (("z+", c_zm, c_xzm, 0, to_zp), ("z-", c_zp, c_xzp, B, to_zm)):
        hid_add("x0" + way, c_xl, 0, A, device)
        hid_add("f0" + way, near, at, B, device)
        hid_add("q0" + way, xnear, at, B, device)
        hid_add("f1" + way, near, A + at, B, device)
        hid_add("n1x" + way, near, A, A, to_xl)
    hid_add("zf1x", c_zf, A, A, to_xl)

    def hid_send(*names):
        for name in names:
            send(hm[name])

    def hid_wait(*names):
        for name in names:
            hm[name].wait_recv()

    hid_send("o1z+", "o1z-", "o0z+", "o0z-")

    loads[3].wait()

    def turn_inp(t, _):
        part = pl.ds(pl.multiple_of(t * 128, 128), 128)
        inp_t[part, rows(r)] = inp_own[:, part].astype(F32).T.astype(BF16)
        return 0

    lax.fori_loop(0, D // 128, turn_inp, 0)

    row_xh(cm)
    hid_send("o0x", "o1x")
    row_near(cm, "o")
    hid_wait("o1z+", "o1z-")
    hid_send("f1z+", "f1z-", "n1xz+", "n1xz-")
    row_near(cm, "h")
    hid_wait("o0x")
    hid_send("x0z+", "x0z-")
    hid_wait("o0z+", "o0z-")
    hid_send("f0z+", "f0z-")
    row_far(cm, "o")
    row_far(cm, "h")
    row_finish(cm)
    loads[4].wait()

    def gh_dot(c_):
        return lax.dot_general(cot[toks(c_), :], wd[...], ACROSS, preferred_element_type=F32)

    gm = {}

    def gh_add(name, i, device):
        gm[name] = message(GH0 + i, gh_send.at[i], gh_recv.at[i], device)

    for k, who in enumerate(("t", "o")):
        gh_add("r+" + who, 0 + k, to_zp)
        gh_add("r-" + who, 2 + k, to_zm)
        gh_add("d+" + who, 4 + k, to_zp)
        gh_add("d-" + who, 6 + k, to_zm)
        gh_add("k+" + who, 8 + k, to_zp)
        gh_add("k-" + who, 10 + k, to_zm)
        gh_add("x%d" % k, 12 + k, to_xl)
    sides = (("t", 0, xo), ("o", 1, xl))

    def gh_start(who, k, x_):
        part = gh_dot(x_ * 4 + z_far).astype(BF16)
        gh_send[0 + k] = part[:HALF]
        gh_send[2 + k] = part[HALF:]
        send(gm["r+" + who])
        send(gm["r-" + who])
        part = gh_dot(x_ * 4 + z_up)
        gh_send[4 + k] = part[HALF:].astype(BF16)
        gh_keep[k] = part[:HALF]
        send(gm["d+" + who])
        part = gh_dot(x_ * 4 + z_dn)
        gh_send[6 + k] = part[:HALF].astype(BF16)
        gh_keep[2 + k] = part[HALF:]
        send(gm["d-" + who])

    def gh_combine(who, k, x_):
        gm["r+" + who].wait_recv()
        gh_send[8 + k] = (gh_keep[k] + gh_recv[0 + k].astype(F32)).astype(BF16)
        send(gm["k+" + who])
        gm["r-" + who].wait_recv()
        gh_send[10 + k] = (gh_keep[2 + k] + gh_recv[2 + k].astype(F32)).astype(BF16)
        send(gm["k-" + who])

    gh_start(*sides[0])
    gh_own[...] = gh_dot(xo * 4 + z)
    row_start(im)
    gh_combine(*sides[0])
    gh_start(*sides[1])
    hid_wait("f1z+", "f1z-")
    hid_send("zf1x")
    row_xh(im)
    row_near(im, "o")
    gm["d+t"].wait_recv()
    gm["d-t"].wait_recv()
    gm["k+t"].wait_recv()
    gm["k-t"].wait_recv()
    gh_send[12] = (
        gh_own[pl.ds(0, HALF), :] + gh_recv[6].astype(F32) + gh_recv[8].astype(F32)
    ).astype(BF16)
    send(gm["x0"])
    gh_send[13] = (
        gh_own[pl.ds(HALF, HALF), :] + gh_recv[4].astype(F32) + gh_recv[10].astype(F32)
    ).astype(BF16)
    send(gm["x1"])
    gh_combine(*sides[1])
    hid_wait("x0z+", "x0z-")
    hid_send("q0z+", "q0z-")
    gh_own[...] = gh_dot(c)
    row_near(im, "h")
    gm["d+o"].wait_recv()
    gm["d-o"].wait_recv()
    gm["k+o"].wait_recv()
    gm["k-o"].wait_recv()

    gg = {}

    def g_add(name, c_, h, start, size, device):
        ref = grads.at[tile(c_ * TOK + h * HALF + start, size, 16), :]
        gg[name] = message(G0 + len(gg), ref, ref, device)

    across_x = HALF - FWD
    for h in (0, 1):
        for way, device in (("z+", to_zp), ("z-", to_zm), ("x", to_xl)):
            g_add("o%dz%s" % (h, way), c, h, 0, FWD, device)
            g_add("o%dx%s" % (h, way), c, h, FWD, across_x, device)
        g_add("x%dz+" % h, c_xl, h, FWD, across_x, to_zp)
        g_add("x%dz-" % h, c_xl, h, FWD, across_x, to_zm)
        g_add("zm%dx" % h, c_zm, h, 0, FWD, to_xl)
        g_add("zp%dx" % h, c_zp, h, 0, FWD, to_xl)
        g_add("zf%dx" % h, c_zf, h, 0, FWD, to_xl)
    for h, way, near, xnear, device in ((0, "z+", c_zm, c_xzm, to_zp), (1, "z-", c_zp, c_xzp, to_zm)):
        g_add("fz" + way, near, h, 0, FWD, device)
        g_add("fx" + way, near, h, FWD, across_x, device)
        g_add("q" + way, xnear, h, FWD, across_x - LATE, device)
        g_add("l" + way, xnear, h, HALF - LATE, LATE, device)

    for h in (0, 1):
        gm["x%d" % h].wait_recv()
        a, b = ((6, 8), (4, 10))[h]

        def grad(t, _, h=h, a=a, b=b):
            here = pl.ds(pl.multiple_of(t * 16, 16), 16)
            part = pl.ds(pl.multiple_of(h * HALF + t * 16, 16), 16)
            gh = (
                gh_own[part, :]
                + gh_recv[a + 1, here, :].astype(F32)
                + gh_recv[b + 1, here, :].astype(F32)
                + gh_recv[12 + h, here, :].astype(F32)
            )
            dst = tile(c * TOK + h * HALF + t * 16, 16, 16)
            grads[dst, pl.ds(0, F)] = (gh * slope[part, :]).astype(BF16)
            grads[dst, pl.ds(F, F)] = (gh * silu[part, :]).astype(BF16)
            return 0

        lax.fori_loop(0, HALF // 16, grad, 0)
        for part in "zx":
            for way in ("z+", "z-", "x"):
                send(gg["o%d%s%s" % (h, part, way)])

    loads[5].wait()
    loads[6].wait()

    pairs = []
    sums = []

    def gi_make(c_, start=0, size=HALF):
        i = len(pairs)
        spot = min(i, 7)
        both = jnp.concatenate(
            [grads[tile(c_ * TOK + h * HALF + start, size, 16), :] for h in (0, 1)], axis=0
        )
        gi_part[i % 2, pl.ds(0, 2 * size), :] = lax.dot_general(
            both, w_in[...], ACROSS, preferred_element_type=F32
        )
        here = pl.ds(start, size)
        theirs = tile((1 - core) * size, size, size)
        pair_send[spot, here, :] = gi_part[i % 2, theirs, :].astype(BF16)
        m = message(PAIR0 + i, pair_send.at[spot, here], pair_recv.at[spot, here], to_core)
        send(m)
        pairs.append((m, c_, start, size))

    def gi_sum():
        i = len(sums)
        spot = min(i, 7)
        m, c_, start, size = pairs[i]
        m.wait_recv()
        mine = tile(core * size, size, size)
        here = pl.ds(start, size)
        q_send[spot, here, :] = (
            gi_part[i % 2, mine, :] + pair_recv[spot, here, :].astype(F32)
        ).astype(BF16)
        y_, xh_ = lax.div(c_, 2), lax.rem(c_, 2)
        arrived = q_late_sem if i == 8 else q_recv_sem
        q = pltpu.make_async_remote_copy(
            src_ref=q_send.at[spot, here],
            dst_ref=q_recv.at[xh_ * 4 + y, here],
            send_sem=q_send_sem.at[i],
            recv_sem=arrived.at[xh_ * 4 + y],
            device_id=(row_of(y_, xh, core), c),
            device_id_type=MESH,
        )
        ours = y_ == y

        @pl.when(jnp.logical_not(ours))
        def _():
            q.start()

        @pl.when(ours)
        def _():
            q_recv[xh_ * 4 + y, here, :] = q_send[spot, here, :]

        sums.append((q, ours))

    def y_total(xh_, start, size, sem, store):
        here = pl.ds(start, size)
        for j in (1, 2, 3):
            slot = xh_ * 4 + lax.rem(y + j, 4)
            pltpu.make_async_remote_copy(
                src_ref=q_send.at[0, here],
                dst_ref=q_recv.at[slot, here],
                send_sem=q_send_sem.at[0],
                recv_sem=sem.at[slot],
                device_id=to_yp,
                device_id_type=MESH,
            ).wait_recv()

        def add(t, _):
            part = pl.ds(pl.multiple_of(start + t * 16, 16), 16)
            total = q_recv[xh_ * 4, part, :].astype(F32)
            for j in (1, 2, 3):
                total = total + q_recv[xh_ * 4 + j, part, :].astype(F32)
            store(part, total)
            return 0

        lax.fori_loop(0, size // 16, add, 0)

    last_xh = c_xzf == y * 2 + xho
    last_own = c_xzf == chip
    parts = (
        (jnp.logical_not(last_xh), 0, HALF, q_recv_sem),
        (last_xh, 0, HALF - LATE, q_recv_sem),
        (last_xh, HALF - LATE, LATE, q_late_sem),
    )
    fwd = []

    def forward(k):
        when, start, size, sem = parts[k]
        here = pl.ds(start, size)
        m = message(FWD0 + k, x_send.at[here], x_recv.at[here], to_xh)
        fwd.append(m)

        @pl.when(when)
        def _():
            def store(part, total):
                x_send[part, :] = total.astype(BF16)

            y_total(xho, start, size, sem, store)
            m.start()

    outs = []

    def down(t, _):
        part = pl.ds(pl.multiple_of(t * 224, 32), 224)
        dwd[part, :] = jnp.dot(
            hid_t[part, :], cot[...], preferred_element_type=F32
        ).astype(BF16)
        return 0

    gi_make(c)
    for name in ("o0zz+", "o0zz-"):
        gg[name].wait_recv()
    send(gg["fzz+"])
    send(gg["zm0x"])
    send(gg["zp0x"])
    hid_wait("f0z+", "f0z-", "q0z+", "q0z-")
    hid_wait("o1x", "n1xz+", "n1xz-", "zf1x")
    lax.fori_loop(0, 2, down, 0)
    row_far(im, "o")
    row_far(im, "h")
    gg["o0xz+"].wait_recv()
    send(gg["fxz+"])
    gg["o0xx"].wait_recv()
    send(gg["x0z+"])
    gg["o1zz+"].wait_recv()
    gg["o1zz-"].wait_recv()
    send(gg["fzz-"])
    send(gg["zm1x"])
    send(gg["zp1x"])
    lax.fori_loop(2, 4, down, 0)
    copy = pltpu.make_async_copy(dwd, dwd_hbm, out_sem.at[0])
    copy.start()
    outs.append(copy)
    gg["o1xz-"].wait_recv()
    send(gg["fxz-"])
    gg["o1xx"].wait_recv()
    send(gg["x1z-"])
    send(gg["x0z-"])
    send(gg["x1z+"])
    gg["fzz+"].wait_recv()
    send(gg["zf0x"])
    gg["fzz-"].wait_recv()
    send(gg["zf1x"])
    gg["o0zx"].wait_recv()
    gg["o1zx"].wait_recv()
    gi_make(c_xl)
    gi_sum()
    gg["o1xz+"].wait_recv()
    gi_make(c_zm)
    gi_sum()
    gg["o0xz-"].wait_recv()
    gi_make(c_zp)
    gi_sum()
    gg["fxz+"].wait_recv()
    gg["fxz-"].wait_recv()
    gi_make(c_zf)
    gi_sum()
    row_finish(im)

    def inward(t, _, x_, first):
        part = pl.ds(pl.multiple_of(t * 256, 256), 256)
        deep = tile(x_ * 1024, 1024, 1024)
        for k in (0, 1):
            part_sum = jnp.dot(
                inp_t[part, deep], grads[deep, pl.ds(k * F, F)], preferred_element_type=F32
            )
            if first:
                dw_sum[k, part, :] = part_sum
            else:
                dw[k, part, :] = (dw_sum[k, part, :] + part_sum).astype(BF16)
        return 0

    lax.fori_loop(0, 2, functools.partial(inward, x_=xl, first=True), 0)
    gg["x0z+"].wait_recv()
    send(gg["qz+"])
    send(gg["lz+"])
    gg["x1z-"].wait_recv()
    send(gg["qz-"])
    send(gg["lz-"])
    lax.fori_loop(2, 4, functools.partial(inward, x_=xl, first=True), 0)
    for h in (0, 1):
        gg["zm%dx" % h].wait_recv()
        gg["zp%dx" % h].wait_recv()
    gg["x1z+"].wait_recv()
    gi_make(c_xzm)
    gi_sum()
    gg["x0z-"].wait_recv()
    gi_make(c_xzp)
    gi_sum()
    for h in (0, 1):
        gg["zf%dx" % h].wait_recv()
    gg["qz+"].wait_recv()
    gg["qz-"].wait_recv()
    gi_make(c_xzf, 0, HALF - LATE)
    gi_sum()
    gg["lz+"].wait_recv()
    gg["lz-"].wait_recv()
    gi_make(c_xzf, HALF - LATE, LATE)
    gi_sum()
    gi_sum()
    forward(0)
    lax.fori_loop(0, 3, functools.partial(inward, x_=xo, first=False), 0)
    forward(1)
    lax.fori_loop(3, 4, functools.partial(inward, x_=xo, first=False), 0)
    forward(2)
    for k, dst in ((0, dwg_hbm), (1, dwu_hbm)):
        copy = pltpu.make_async_copy(dw.at[k], dst, out_sem.at[1 + k])
        copy.start()
        outs.append(copy)

    def finish(part, total):
        gi_out[part, :] = (total + x_recv[part, :].astype(F32)).astype(BF16)

    @pl.when(jnp.logical_not(last_own))
    def _():
        fwd[0].wait_recv()
        y_total(xh, 0, HALF, q_recv_sem, finish)

    @pl.when(last_own)
    def _():
        fwd[1].wait_recv()
        y_total(xh, 0, HALF - LATE, q_recv_sem, finish)
        fwd[2].wait_recv()
        y_total(xh, HALF - LATE, LATE, q_late_sem, finish)

    copy = pltpu.make_async_copy(gi_out, gi_hbm, out_sem.at[3])
    copy.start()
    outs.append(copy)
    for m in started:
        m.wait_send()
    for m, part in zip(fwd, parts):

        @pl.when(part[0])
        def _():
            m.wait_send()

    for q, ours in sums:

        @pl.when(jnp.logical_not(ours))
        def _():
            q.wait_send()

    for copy in outs:
        copy.wait()


def write_out(*refs):
    sources, targets, held = refs[:4], refs[4:8], refs[8:12]
    load_sem, store_sem = refs[12:]
    loads, stores = [], []
    for src, mid, dst in zip(sources, held, targets):
        step = src.shape[0] // PARTS
        for k in range(PARTS):
            here = pl.ds(k * step, step)
            i = len(loads)
            loads.append(pltpu.make_async_copy(src.at[here, :], mid.at[here, :], load_sem.at[i]))
            stores.append(pltpu.make_async_copy(mid.at[here, :], dst.at[here, :], store_sem.at[i]))
    for load in loads:
        load.start()
    for load, store in zip(loads, stores):
        load.wait()
        store.start()
    for store in stores:
        store.wait()


def shards(inputs, cotangent, gate_pre, up_pre, w_gate, w_up, w_down):
    anywhere = pl.BlockSpec(memory_space=pl.ANY)
    vmem = pltpu.VMEM
    dma = pltpu.SemaphoreType.DMA
    done = pl.pallas_call(
        kernel,
        out_shape=(
            jax.ShapeDtypeStruct((ROWS, D), BF16),
            jax.ShapeDtypeStruct((D, F), BF16),
            jax.ShapeDtypeStruct((D, F), BF16),
            jax.ShapeDtypeStruct((F, D), BF16),
        ),
        in_specs=[anywhere] * 7,
        out_specs=(anywhere,) * 4,
        scratch_shapes=[
            vmem((2048, D), BF16),
            vmem((D, 2048), BF16),
            vmem((F, 2048), BF16),
            vmem((2048, 2 * F), BF16),
            vmem((D, 2 * F), BF16),
            vmem((F, D), BF16),
            vmem((ROWS, D), BF16),
            vmem((TOK, F), BF16),
            vmem((TOK, F), BF16),
            vmem((TOK, F), F32),
            vmem((TOK, F), F32),
            vmem((14, HALF, F), BF16),
            vmem((14, HALF, F), BF16),
            vmem((4, HALF, F), F32),
            vmem((TOK, F), F32),
            vmem((2, TOK, D), F32),
            vmem((8, ROWS, D), BF16),
            vmem((8, ROWS, D), BF16),
            vmem((8, ROWS, D), BF16),
            vmem((8, ROWS, D), BF16),
            vmem((ROWS, D), BF16),
            vmem((ROWS, D), BF16),
            vmem((2, D, F), BF16),
            vmem((2, D, F), F32),
            vmem((F, D), BF16),
            vmem((ROWS, D), BF16),
            dma((N_SEM,)),
            dma((N_SEM,)),
            dma((9,)),
            dma((8,)),
            dma((8,)),
            dma((7,)),
            dma((4,)),
        ],
        compiler_params=pltpu.CompilerParams(
            collective_id=0, has_side_effects=True, vmem_limit_bytes=60 * 2**20
        ),
    )(inputs, cotangent, gate_pre, up_pre, w_gate, w_up, w_down)
    return pl.pallas_call(
        write_out,
        out_shape=tuple(jax.ShapeDtypeStruct(x.shape, BF16) for x in done),
        in_specs=[anywhere] * 4,
        out_specs=(anywhere,) * 4,
        scratch_shapes=[vmem(x.shape, BF16) for x in done] + [dma((4 * PARTS,))] * 2,
        compiler_params=pltpu.CompilerParams(vmem_limit_bytes=60 * 2**20),
    )(*done)


def solution(mesh):
    placed = (
        P("row", "col"),
        P("row", "col"),
        P("col", "row"),
        P("col", "row"),
        P("col", "row"),
        P("col", "row"),
        P("row", "col"),
    )
    return jax.shard_map(
        shards,
        mesh=mesh,
        in_specs=placed,
        out_specs=(P("row", "col"), P("col", "row"), P("col", "row"), P("row", "col")),
        check_vma=False,
    )
```

```python
import functools

import jax
import jax.numpy as jnp
from jax import lax
from jax.experimental import pallas as pl
from jax.experimental.pallas import tpu as pltpu
from jax.sharding import PartitionSpec as P

MESH = pl.DeviceIdType.MESH
BF16 = jnp.bfloat16
F32 = jnp.float32
ACROSS = (((1,), (1,)), ((), ()))

ROWS = 128
TOK = 256
HALF = 128
FWD = 48
LATE = 32
D = 1024
F = 896

N_ROWS = 17
N_HID = 17
N_GH = 14
N_G = 30
COT0 = 0
INP0 = COT0 + N_ROWS
HID0 = INP0 + N_ROWS
GH0 = HID0 + N_HID
G0 = GH0 + N_GH
PAIR0 = G0 + N_G
N_FWD = 3
FWD0 = PAIR0 + 9
N_SEM = FWD0 + N_FWD
PARTS = 8


def kernel(
    inp_hbm, cot_hbm, gate_hbm, up_hbm, wg_hbm, wu_hbm, wd_hbm,
    gi_hbm, dwg_hbm, dwu_hbm, dwd_hbm,
    cot, inp_t, hid_t, grads, w_in, wd, inp_own, gate, up,
    slope, silu, gh_send, gh_recv, gh_keep, gh_own,
    gi_part, pair_send, pair_recv, q_send, q_recv, x_send, x_recv,
    dw, dw_sum, dwd, gi_out,
    send_sem, recv_sem, q_send_sem, q_recv_sem, q_late_sem, local_sem, out_sem,
):
    r = lax.axis_index("row")
    c = lax.axis_index("col")
    core = lax.rem(r, 2)
    chip = lax.div(r, 2)
    xh = lax.rem(chip, 2)
    y = lax.div(chip, 2)
    xl = lax.div(c, 4)
    z = lax.rem(c, 4)

    def row_of(y_, xh_, core_):
        return (y_ * 2 + xh_) * 2 + core_

    y_up, y_dn, y_far = lax.rem(y + 1, 4), lax.rem(y + 3, 4), lax.rem(y + 2, 4)
    z_up, z_dn, z_far = lax.rem(z + 1, 4), lax.rem(z + 3, 4), lax.rem(z + 2, 4)
    xo = 1 - xl
    xho = 1 - xh
    c_xl = xo * 4 + z

    to_yp = (row_of(y_up, xh, core), c)
    to_ym = (row_of(y_dn, xh, core), c)
    to_xh = (row_of(y, xho, core), c)
    to_core = (row_of(y, xh, 1 - core), c)
    to_zp = (r, xl * 4 + z_up)
    to_zm = (r, xl * 4 + z_dn)
    to_xl = (r, c_xl)

    def local(i, src, dst):
        return pltpu.make_async_copy(src, dst, local_sem.at[i])

    def tile(start, size, step):
        return pl.ds(pl.multiple_of(start, step), size)

    def rows(r_):
        return tile(r_ * ROWS, ROWS, ROWS)

    def toks(c_):
        return tile(c_ * TOK, TOK, TOK)

    def halves(c_, h):
        return tile(c_ * TOK + h * HALF, HALF, HALF)

    loads = [
        local(0, cot_hbm, cot.at[rows(r), :]),
        local(1, gate_hbm, gate),
        local(2, up_hbm, up),
        local(3, inp_hbm, inp_own),
        local(4, wd_hbm, wd),
        local(5, wg_hbm, w_in.at[:, pl.ds(0, F)]),
        local(6, wu_hbm, w_in.at[:, pl.ds(F, F)]),
    ]
    for load in loads:
        load.start()

    barrier = pltpu.get_barrier_semaphore()
    partners = [to_yp, to_ym, to_xh, to_core, to_zp, to_zm, to_xl]
    for device in partners:
        pl.semaphore_signal(barrier, inc=1, device_id=device, device_id_type=MESH)
    far = [
        (row_of(y_far, xh, core), c),
        (row_of(y_up, xho, core), c),
        (row_of(y_dn, xho, core), c),
        (row_of(y_far, xho, core), c),
    ]
    for device in far:
        pl.semaphore_signal(barrier, inc=1, device_id=device, device_id_type=MESH)
    pl.semaphore_wait(barrier, len(partners) + len(far))

    started = []

    def message(i, src, dst, device):
        return pltpu.make_async_remote_copy(
            src_ref=src,
            dst_ref=dst,
            send_sem=send_sem.at[i],
            recv_sem=recv_sem.at[i],
            device_id=device,
            device_id_type=MESH,
        )

    def send(m):
        m.start()
        started.append(m)

    def row_gather(base, at):
        m = {}

        def add(name, i, y_, xh_, part, device):
            ref = at(y_, xh_, part)
            m[name] = message(base + i, ref, ref, device)

        add("oh", 0, y, xh, None, to_xh)
        add("oy+", 1, y, xh, None, to_yp)
        add("oy-", 2, y, xh, None, to_ym)
        add("hy+", 3, y, xho, None, to_yp)
        add("hy-", 4, y, xho, None, to_ym)
        add("o2y+", 5, y_dn, xh, 0, to_yp)
        add("o2y-", 6, y_up, xh, 1, to_ym)
        add("h2y+", 7, y_dn, xho, 0, to_yp)
        add("h2y-", 8, y_up, xho, 1, to_ym)
        k = 9
        for yn, y_ in (("0", y), ("-", y_dn), ("+", y_up), ("f", y_far)):
            for xn, xh_ in (("o", xh), ("h", xho)):
                add(xn + yn + "c", k, y_, xh_, None, to_core)
                k += 1
        return m

    def cot_at(y_, xh_, part):
        start = row_of(y_, xh_, core) * ROWS
        if part is None:
            return cot.at[tile(start, ROWS, ROWS), :]
        return cot.at[tile(start + part * (ROWS // 2), ROWS // 2, ROWS // 2), :]

    def inp_at(y_, xh_, part):
        cols = tile(row_of(y_, xh_, core) * ROWS, ROWS, ROWS)
        if part is None:
            return inp_t.at[:, cols]
        return inp_t.at[pl.ds(part * (D // 2), D // 2), cols]

    cm = row_gather(COT0, cot_at)
    im = row_gather(INP0, inp_at)

    def row_start(m):
        send(m["oh"])
        send(m["oy+"])
        send(m["oy-"])
        send(m["o0c"])

    def row_xh(m):
        m["oh"].wait_recv()
        send(m["hy+"])
        send(m["hy-"])
        send(m["h0c"])

    def row_near(m, which):
        m[which + "y+"].wait_recv()
        send(m[which + "2y+"])
        send(m[which + "-c"])
        m[which + "y-"].wait_recv()
        send(m[which + "2y-"])
        send(m[which + "+c"])

    def row_far(m, which):
        m[which + "2y+"].wait_recv()
        m[which + "2y-"].wait_recv()
        send(m[which + "fc"])

    def row_finish(m):
        for name in m:
            if name.endswith("c"):
                m[name].wait_recv()

    loads[0].wait()
    row_start(cm)
    loads[1].wait()
    loads[2].wait()

    def activate(t, _):
        part = pl.ds(pl.multiple_of(t * 16, 16), 16)
        g = gate[part, :].astype(F32)
        u = up[part, :].astype(F32)
        s = 1.0 / (1.0 + jnp.exp(-g))
        sl = g * s
        silu[part, :] = sl
        slope[part, :] = u * s * (1.0 + g * (1.0 - s))
        gh_own[part, :] = sl * u
        return 0

    lax.fori_loop(0, TOK // 16, activate, 0)

    def turn(t, _):
        part = pl.ds(pl.multiple_of(t * 128, 128), 128)
        hid_t[part, toks(c)] = gh_own[:, part].T.astype(BF16)
        return 0

    lax.fori_loop(0, F // 128, turn, 0)

    def hid_add(name, c_, start, size, device):
        ref = hid_t.at[pl.ds(start, size), toks(c_)]
        hm[name] = message(HID0 + len(hm), ref, ref, device)

    hm = {}
    c_zp, c_zm, c_zf = xl * 4 + z_up, xl * 4 + z_dn, xl * 4 + z_far
    c_xzp, c_xzm, c_xzf = xo * 4 + z_up, xo * 4 + z_dn, xo * 4 + z_far
    A, B = F // 2, F // 4
    for way, device in (("z+", to_zp), ("z-", to_zm), ("x", to_xl)):
        hid_add("o0" + way, c, 0, A, device)
        hid_add("o1" + way, c, A, A, device)
    for way, near, xnear, at, device in (("z+", c_zm, c_xzm, 0, to_zp), ("z-", c_zp, c_xzp, B, to_zm)):
        hid_add("x0" + way, c_xl, 0, A, device)
        hid_add("f0" + way, near, at, B, device)
        hid_add("q0" + way, xnear, at, B, device)
        hid_add("f1" + way, near, A + at, B, device)
        hid_add("n1x" + way, near, A, A, to_xl)
    hid_add("zf1x", c_zf, A, A, to_xl)

    def hid_send(*names):
        for name in names:
            send(hm[name])

    def hid_wait(*names):
        for name in names:
            hm[name].wait_recv()

    hid_send("o1z+", "o1z-", "o0z+", "o0z-")

    loads[3].wait()

    def turn_inp(t, _):
        part = pl.ds(pl.multiple_of(t * 128, 128), 128)
        inp_t[part, rows(r)] = inp_own[:, part].astype(F32).T.astype(BF16)
        return 0

    lax.fori_loop(0, D // 128, turn_inp, 0)

    row_xh(cm)
    hid_send("o0x", "o1x")
    row_near(cm, "o")
    hid_wait("o1z+", "o1z-")
    hid_send("f1z+", "f1z-", "n1xz+", "n1xz-")
    row_near(cm, "h")
    hid_wait("o0x")
    hid_send("x0z+", "x0z-")
    hid_wait("o0z+", "o0z-")
    hid_send("f0z+", "f0z-")
    row_far(cm, "o")
    row_far(cm, "h")
    row_finish(cm)
    loads[4].wait()

    def gh_dot(c_):
        return lax.dot_general(cot[toks(c_), :], wd[...], ACROSS, preferred_element_type=F32)

    gm = {}

    def gh_add(name, i, device):
        gm[name] = message(GH0 + i, gh_send.at[i], gh_recv.at[i], device)

    for k, who in enumerate(("t", "o")):
        gh_add("r+" + who, 0 + k, to_zp)
        gh_add("r-" + who, 2 + k, to_zm)
        gh_add("d+" + who, 4 + k, to_zp)
        gh_add("d-" + who, 6 + k, to_zm)
        gh_add("k+" + who, 8 + k, to_zp)
        gh_add("k-" + who, 10 + k, to_zm)
        gh_add("x%d" % k, 12 + k, to_xl)
    sides = (("t", 0, xo), ("o", 1, xl))

    def gh_start(who, k, x_):
        part = gh_dot(x_ * 4 + z_far).astype(BF16)
        gh_send[0 + k] = part[:HALF]
        gh_send[2 + k] = part[HALF:]
        send(gm["r+" + who])
        send(gm["r-" + who])
        part = gh_dot(x_ * 4 + z_up)
        gh_send[4 + k] = part[HALF:].astype(BF16)
        gh_keep[k] = part[:HALF]
        send(gm["d+" + who])
        part = gh_dot(x_ * 4 + z_dn)
        gh_send[6 + k] = part[:HALF].astype(BF16)
        gh_keep[2 + k] = part[HALF:]
        send(gm["d-" + who])

    def gh_combine(who, k, x_):
        gm["r+" + who].wait_recv()
        gh_send[8 + k] = (gh_keep[k] + gh_recv[0 + k].astype(F32)).astype(BF16)
        send(gm["k+" + who])
        gm["r-" + who].wait_recv()
        gh_send[10 + k] = (gh_keep[2 + k] + gh_recv[2 + k].astype(F32)).astype(BF16)
        send(gm["k-" + who])

    gh_start(*sides[0])
    gh_own[...] = gh_dot(xo * 4 + z)
    row_start(im)
    gh_combine(*sides[0])
    gh_start(*sides[1])
    hid_wait("f1z+", "f1z-")
    hid_send("zf1x")
    row_xh(im)
    row_near(im, "o")
    gm["d+t"].wait_recv()
    gm["d-t"].wait_recv()
    gm["k+t"].wait_recv()
    gm["k-t"].wait_recv()
    gh_send[12] = (
        gh_own[pl.ds(0, HALF), :] + gh_recv[6].astype(F32) + gh_recv[8].astype(F32)
    ).astype(BF16)
    send(gm["x0"])
    gh_send[13] = (
        gh_own[pl.ds(HALF, HALF), :] + gh_recv[4].astype(F32) + gh_recv[10].astype(F32)
    ).astype(BF16)
    send(gm["x1"])
    gh_combine(*sides[1])
    hid_wait("x0z+", "x0z-")
    hid_send("q0z+", "q0z-")
    gh_own[...] = gh_dot(c)
    row_near(im, "h")
    gm["d+o"].wait_recv()
    gm["d-o"].wait_recv()
    gm["k+o"].wait_recv()
    gm["k-o"].wait_recv()

    gg = {}

    def g_add(name, c_, h, start, size, device):
        ref = grads.at[tile(c_ * TOK + h * HALF + start, size, 16), :]
        gg[name] = message(G0 + len(gg), ref, ref, device)

    across_x = HALF - FWD
    for h in (0, 1):
        for way, device in (("z+", to_zp), ("z-", to_zm), ("x", to_xl)):
            g_add("o%dz%s" % (h, way), c, h, 0, FWD, device)
            g_add("o%dx%s" % (h, way), c, h, FWD, across_x, device)
        g_add("x%dz+" % h, c_xl, h, FWD, across_x, to_zp)
        g_add("x%dz-" % h, c_xl, h, FWD, across_x, to_zm)
        g_add("zm%dx" % h, c_zm, h, 0, FWD, to_xl)
        g_add("zp%dx" % h, c_zp, h, 0, FWD, to_xl)
        g_add("zf%dx" % h, c_zf, h, 0, FWD, to_xl)
    for h, way, near, xnear, device in ((0, "z+", c_zm, c_xzm, to_zp), (1, "z-", c_zp, c_xzp, to_zm)):
        g_add("fz" + way, near, h, 0, FWD, device)
        g_add("fx" + way, near, h, FWD, across_x, device)
        g_add("q" + way, xnear, h, FWD, across_x - LATE, device)
        g_add("l" + way, xnear, h, HALF - LATE, LATE, device)

    for h in (0, 1):
        gm["x%d" % h].wait_recv()
        a, b = ((6, 8), (4, 10))[h]

        def grad(t, _, h=h, a=a, b=b):
            here = pl.ds(pl.multiple_of(t * 16, 16), 16)
            part = pl.ds(pl.multiple_of(h * HALF + t * 16, 16), 16)
            gh = (
                gh_own[part, :]
                + gh_recv[a + 1, here, :].astype(F32)
                + gh_recv[b + 1, here, :].astype(F32)
                + gh_recv[12 + h, here, :].astype(F32)
            )
            dst = tile(c * TOK + h * HALF + t * 16, 16, 16)
            grads[dst, pl.ds(0, F)] = (gh * slope[part, :]).astype(BF16)
            grads[dst, pl.ds(F, F)] = (gh * silu[part, :]).astype(BF16)
            return 0

        lax.fori_loop(0, HALF // 16, grad, 0)
        for part in "zx":
            for way in ("z+", "z-", "x"):
                send(gg["o%d%s%s" % (h, part, way)])

    loads[5].wait()
    loads[6].wait()

    pairs = []
    sums = []

    def gi_make(c_, start=0, size=HALF):
        i = len(pairs)
        spot = min(i, 7)
        both = jnp.concatenate(
            [grads[tile(c_ * TOK + h * HALF + start, size, 16), :] for h in (0, 1)], axis=0
        )
        gi_part[i % 2, pl.ds(0, 2 * size), :] = lax.dot_general(
            both, w_in[...], ACROSS, preferred_element_type=F32
        )
        here = pl.ds(start, size)
        theirs = tile((1 - core) * size, size, size)
        pair_send[spot, here, :] = gi_part[i % 2, theirs, :].astype(BF16)
        m = message(PAIR0 + i, pair_send.at[spot, here], pair_recv.at[spot, here], to_core)
        send(m)
        pairs.append((m, c_, start, size))

    def gi_sum():
        i = len(sums)
        spot = min(i, 7)
        m, c_, start, size = pairs[i]
        m.wait_recv()
        mine = tile(core * size, size, size)
        here = pl.ds(start, size)
        q_send[spot, here, :] = (
            gi_part[i % 2, mine, :] + pair_recv[spot, here, :].astype(F32)
        ).astype(BF16)
        y_, xh_ = lax.div(c_, 2), lax.rem(c_, 2)
        arrived = q_late_sem if i == 8 else q_recv_sem
        q = pltpu.make_async_remote_copy(
            src_ref=q_send.at[spot, here],
            dst_ref=q_recv.at[xh_ * 4 + y, here],
            send_sem=q_send_sem.at[i],
            recv_sem=arrived.at[xh_ * 4 + y],
            device_id=(row_of(y_, xh, core), c),
            device_id_type=MESH,
        )
        ours = y_ == y

        @pl.when(jnp.logical_not(ours))
        def _():
            q.start()

        @pl.when(ours)
        def _():
            q_recv[xh_ * 4 + y, here, :] = q_send[spot, here, :]

        sums.append((q, ours))

    def y_total(xh_, start, size, sem, store):
        here = pl.ds(start, size)
        for j in (1, 2, 3):
            slot = xh_ * 4 + lax.rem(y + j, 4)
            pltpu.make_async_remote_copy(
                src_ref=q_send.at[0, here],
                dst_ref=q_recv.at[slot, here],
                send_sem=q_send_sem.at[0],
                recv_sem=sem.at[slot],
                device_id=to_yp,
                device_id_type=MESH,
            ).wait_recv()

        def add(t, _):
            part = pl.ds(pl.multiple_of(start + t * 16, 16), 16)
            total = q_recv[xh_ * 4, part, :].astype(F32)
            for j in (1, 2, 3):
                total = total + q_recv[xh_ * 4 + j, part, :].astype(F32)
            store(part, total)
            return 0

        lax.fori_loop(0, size // 16, add, 0)

    last_xh = c_xzf == y * 2 + xho
    last_own = c_xzf == chip
    parts = (
        (jnp.logical_not(last_xh), 0, HALF, q_recv_sem),
        (last_xh, 0, HALF - LATE, q_recv_sem),
        (last_xh, HALF - LATE, LATE, q_late_sem),
    )
    fwd = []

    def forward(k):
        when, start, size, sem = parts[k]
        here = pl.ds(start, size)
        m = message(FWD0 + k, x_send.at[here], x_recv.at[here], to_xh)
        fwd.append(m)

        @pl.when(when)
        def _():
            def store(part, total):
                x_send[part, :] = total.astype(BF16)

            y_total(xho, start, size, sem, store)
            m.start()

    outs = []

    def down(t, _):
        part = pl.ds(pl.multiple_of(t * 224, 32), 224)
        dwd[part, :] = jnp.dot(
            hid_t[part, :], cot[...], preferred_element_type=F32
        ).astype(BF16)
        return 0

    gi_make(c)
    for name in ("o0zz+", "o0zz-"):
        gg[name].wait_recv()
    send(gg["fzz+"])
    send(gg["zm0x"])
    send(gg["zp0x"])
    hid_wait("f0z+", "f0z-", "q0z+", "q0z-")
    hid_wait("o1x", "n1xz+", "n1xz-", "zf1x")
    lax.fori_loop(0, 2, down, 0)
    row_far(im, "o")
    row_far(im, "h")
    gg["o0xz+"].wait_recv()
    send(gg["fxz+"])
    gg["o0xx"].wait_recv()
    send(gg["x0z+"])
    gg["o1zz+"].wait_recv()
    gg["o1zz-"].wait_recv()
    send(gg["fzz-"])
    send(gg["zm1x"])
    send(gg["zp1x"])
    lax.fori_loop(2, 4, down, 0)
    copy = pltpu.make_async_copy(dwd, dwd_hbm, out_sem.at[0])
    copy.start()
    outs.append(copy)
    gg["o1xz-"].wait_recv()
    send(gg["fxz-"])
    gg["o1xx"].wait_recv()
    send(gg["x1z-"])
    send(gg["x0z-"])
    send(gg["x1z+"])
    gg["fzz+"].wait_recv()
    send(gg["zf0x"])
    gg["fzz-"].wait_recv()
    send(gg["zf1x"])
    gg["o0zx"].wait_recv()
    gg["o1zx"].wait_recv()
    gi_make(c_xl)
    gi_sum()
    gg["o1xz+"].wait_recv()
    gi_make(c_zm)
    gi_sum()
    gg["o0xz-"].wait_recv()
    gi_make(c_zp)
    gi_sum()
    gg["fxz+"].wait_recv()
    gg["fxz-"].wait_recv()
    gi_make(c_zf)
    gi_sum()
    row_finish(im)

    def inward(t, _, x_, first):
        part = pl.ds(pl.multiple_of(t * 256, 256), 256)
        deep = tile(x_ * 1024, 1024, 1024)
        for k in (0, 1):
            part_sum = jnp.dot(
                inp_t[part, deep], grads[deep, pl.ds(k * F, F)], preferred_element_type=F32
            )
            if first:
                dw_sum[k, part, :] = part_sum
            else:
                dw[k, part, :] = (dw_sum[k, part, :] + part_sum).astype(BF16)
        return 0

    lax.fori_loop(0, 2, functools.partial(inward, x_=xl, first=True), 0)
    gg["x0z+"].wait_recv()
    send(gg["qz+"])
    send(gg["lz+"])
    gg["x1z-"].wait_recv()
    send(gg["qz-"])
    send(gg["lz-"])
    lax.fori_loop(2, 4, functools.partial(inward, x_=xl, first=True), 0)
    for h in (0, 1):
        gg["zm%dx" % h].wait_recv()
        gg["zp%dx" % h].wait_recv()
    gg["x1z+"].wait_recv()
    gi_make(c_xzm)
    gi_sum()
    gg["x0z-"].wait_recv()
    gi_make(c_xzp)
    gi_sum()
    for h in (0, 1):
        gg["zf%dx" % h].wait_recv()
    gg["qz+"].wait_recv()
    gg["qz-"].wait_recv()
    gi_make(c_xzf, 0, HALF - LATE)
    gi_sum()
    gi_sum()
    gg["lz+"].wait_recv()
    gg["lz-"].wait_recv()
    gi_make(c_xzf, HALF - LATE, LATE)
    gi_sum()
    forward(0)
    lax.fori_loop(0, 3, functools.partial(inward, x_=xo, first=False), 0)
    forward(1)
    lax.fori_loop(3, 4, functools.partial(inward, x_=xo, first=False), 0)
    forward(2)
    for k, dst in ((0, dwg_hbm), (1, dwu_hbm)):
        copy = pltpu.make_async_copy(dw.at[k], dst, out_sem.at[1 + k])
        copy.start()
        outs.append(copy)

    def finish(part, total):
        gi_out[part, :] = (total + x_recv[part, :].astype(F32)).astype(BF16)

    @pl.when(jnp.logical_not(last_own))
    def _():
        fwd[0].wait_recv()
        y_total(xh, 0, HALF, q_recv_sem, finish)

    @pl.when(last_own)
    def _():
        fwd[1].wait_recv()
        y_total(xh, 0, HALF - LATE, q_recv_sem, finish)
        fwd[2].wait_recv()
        y_total(xh, HALF - LATE, LATE, q_late_sem, finish)

    copy = pltpu.make_async_copy(gi_out, gi_hbm, out_sem.at[3])
    copy.start()
    outs.append(copy)
    for m in started:
        m.wait_send()
    for m, part in zip(fwd, parts):

        @pl.when(part[0])
        def _():
            m.wait_send()

    for q, ours in sums:

        @pl.when(jnp.logical_not(ours))
        def _():
            q.wait_send()

    for copy in outs:
        copy.wait()


def write_out(*refs):
    sources, targets, held = refs[:4], refs[4:8], refs[8:12]
    load_sem, store_sem = refs[12:]
    loads, stores = [], []
    for src, mid, dst in zip(sources, held, targets):
        step = src.shape[0] // PARTS
        for k in range(PARTS):
            here = pl.ds(k * step, step)
            i = len(loads)
            loads.append(pltpu.make_async_copy(src.at[here, :], mid.at[here, :], load_sem.at[i]))
            stores.append(pltpu.make_async_copy(mid.at[here, :], dst.at[here, :], store_sem.at[i]))
    for load in loads:
        load.start()
    for load, store in zip(loads, stores):
        load.wait()
        store.start()
    for store in stores:
        store.wait()


def shards(inputs, cotangent, gate_pre, up_pre, w_gate, w_up, w_down):
    anywhere = pl.BlockSpec(memory_space=pl.ANY)
    vmem = pltpu.VMEM
    dma = pltpu.SemaphoreType.DMA
    done = pl.pallas_call(
        kernel,
        out_shape=(
            jax.ShapeDtypeStruct((ROWS, D), BF16),
            jax.ShapeDtypeStruct((D, F), BF16),
            jax.ShapeDtypeStruct((D, F), BF16),
            jax.ShapeDtypeStruct((F, D), BF16),
        ),
        in_specs=[anywhere] * 7,
        out_specs=(anywhere,) * 4,
        scratch_shapes=[
            vmem((2048, D), BF16),
            vmem((D, 2048), BF16),
            vmem((F, 2048), BF16),
            vmem((2048, 2 * F), BF16),
            vmem((D, 2 * F), BF16),
            vmem((F, D), BF16),
            vmem((ROWS, D), BF16),
            vmem((TOK, F), BF16),
            vmem((TOK, F), BF16),
            vmem((TOK, F), F32),
            vmem((TOK, F), F32),
            vmem((14, HALF, F), BF16),
            vmem((14, HALF, F), BF16),
            vmem((4, HALF, F), F32),
            vmem((TOK, F), F32),
            vmem((2, TOK, D), F32),
            vmem((8, ROWS, D), BF16),
            vmem((8, ROWS, D), BF16),
            vmem((8, ROWS, D), BF16),
            vmem((8, ROWS, D), BF16),
            vmem((ROWS, D), BF16),
            vmem((ROWS, D), BF16),
            vmem((2, D, F), BF16),
            vmem((2, D, F), F32),
            vmem((F, D), BF16),
            vmem((ROWS, D), BF16),
            dma((N_SEM,)),
            dma((N_SEM,)),
            dma((9,)),
            dma((8,)),
            dma((8,)),
            dma((7,)),
            dma((4,)),
        ],
        compiler_params=pltpu.CompilerParams(
            collective_id=0, has_side_effects=True, vmem_limit_bytes=60 * 2**20
        ),
    )(inputs, cotangent, gate_pre, up_pre, w_gate, w_up, w_down)
    return pl.pallas_call(
        write_out,
        out_shape=tuple(jax.ShapeDtypeStruct(x.shape, BF16) for x in done),
        in_specs=[anywhere] * 4,
        out_specs=(anywhere,) * 4,
        scratch_shapes=[vmem(x.shape, BF16) for x in done] + [dma((4 * PARTS,))] * 2,
        compiler_params=pltpu.CompilerParams(vmem_limit_bytes=60 * 2**20),
    )(*done)


def solution(mesh):
    placed = (
        P("row", "col"),
        P("row", "col"),
        P("col", "row"),
        P("col", "row"),
        P("col", "row"),
        P("col", "row"),
        P("row", "col"),
    )
    return jax.shard_map(
        shards,
        mesh=mesh,
        in_specs=placed,
        out_specs=(P("row", "col"), P("col", "row"), P("col", "row"), P("row", "col")),
        check_vma=False,
    )
```
